32 devices in a mesh: row: 8 (over y, x, core), col: 4 (over z).
Axes of the slice: x: 2, y: 2, z: 4, core: 2. Of those that a mesh axis runs over, the one named last changes fastest.
Arguments:
- covariance: float32 [12288, 12288], P('row', 'col'), may hold values from -6 to 6
- east_wind: float32 [96, 128], replicated, may hold values from -0.3 to 0.3
- north_wind: float32 [96, 128], replicated, may hold values from -0.3 to 0.3
- diffuse_lon: float32 [96, 128], replicated, may hold values from 0.05 to 0.2
- diffuse_lat: float32 [96, 128], replicated, may hold values from 0.05 to 0.2
Outputs:
- propagated: float32 [12288, 12288], P('row', 'col')
The draws below stay inside these ranges and needn't reach their ends.
All inputs are finite; a program needn't handle non-finite values.
Results may differ from the reference program's by a relative error of at most 0.00002.
Values sent between devices are 32-bit elements; how exact they have to be, the bound alone decides.
A program may use at most 192 MiB of HBM per device.

```python
import math
import jax
import jax.numpy as jnp
from jax import lax

NLAT = 96
NLON = 128
STEPS = 3
ORDER = 12288


def level_of(stream_key, dims, pieces, low, top_value):
    loudness = 1.0
    for axis_at, parts in pieces:
        steps = jax.random.uniform(jax.random.fold_in(jax.random.fold_in(stream_key, 6), axis_at), (parts,), jnp.float32, low / len(pieces), top_value / len(pieces))
        loudness = loudness * jnp.repeat(jnp.exp(steps), dims[axis_at] // parts).reshape((-1,) + (1,) * (len(dims) - 1 - axis_at))
    return loudness


def scatter_about(own_key, dims, scale, limit, pieces=(), held_as=jnp.bfloat16):
    values = jax.random.normal(own_key, dims, jnp.float32) * scale
    if len(pieces) > 0:
        values = level_of(own_key, dims, pieces, -0.22, 0.18) * values
    return jnp.clip(values, min=-limit, max=limit).astype(held_as)


def setup_inputs(seed: int = 0) -> dict:
    keys = jax.random.split(jax.random.key(seed), 6)
    covariance = scatter_about(keys[0], (ORDER, ORDER), 1.0, 6.0, ((0, 8), (1, 4)), jnp.float32)
    east_wind = jnp.clip(jax.random.uniform(keys[1], (NLAT, NLON), jnp.float32, -0.3, 0.3), -0.3, 0.3)
    north_wind = jnp.clip(jax.random.uniform(keys[2], (NLAT, NLON), jnp.float32, -0.3, 0.3), -0.3, 0.3)
    diffuse_lon = jnp.clip(jnp.exp(jax.random.uniform(keys[3], (NLAT, NLON), jnp.float32, math.log(0.05), math.log(0.2))), 0.05, 0.2)
    diffuse_lat = jnp.clip(jnp.exp(jax.random.uniform(keys[4], (NLAT, NLON), jnp.float32, math.log(0.05), math.log(0.2))), 0.05, 0.2)
    return dict(covariance=covariance, east_wind=east_wind, north_wind=north_wind, diffuse_lon=diffuse_lon, diffuse_lat=diffuse_lat)


def advect(widened, lat_dim, east_wind, north_wind, diffuse_lon, diffuse_lat):
    length = widened.shape[lat_dim]
    north = lax.slice_in_dim(widened, 2, length, axis=lat_dim)
    south = lax.slice_in_dim(widened, 0, length - 2, axis=lat_dim)
    center = lax.slice_in_dim(widened, 1, length - 1, axis=lat_dim)
    eastern = jnp.roll(center, -1, lat_dim + 1)
    western = jnp.roll(center, 1, lat_dim + 1)
    return (center - 0.5 * east_wind * (eastern - western) - 0.5 * north_wind * (north - south)
            + diffuse_lon * (eastern - 2.0 * center + western)
            + diffuse_lat * (north - 2.0 * center + south))


def reference(covariance, east_wind, north_wind, diffuse_lon, diffuse_lat):
    values = covariance.reshape(NLAT, NLON, ORDER)
    coefs = [c[:, :, None] for c in (east_wind, north_wind, diffuse_lon, diffuse_lat)]
    for section in range(STEPS):
        widened = jnp.pad(values, ((1, 1), (0, 0), (0, 0)))
        values = advect(widened, 0, *coefs)
    values = values.reshape(ORDER, NLAT, NLON)
    coefs = [c[None] for c in (east_wind, north_wind, diffuse_lon, diffuse_lat)]
    for section in range(STEPS):
        widened = jnp.pad(values, ((0, 0), (1, 1), (0, 0)))
        values = advect(widened, 1, *coefs)
    return values.reshape(ORDER, ORDER)
```

```python
import functools

import jax
import jax.numpy as jnp
from jax import lax
from jax.experimental import pallas as pl
from jax.experimental.pallas import tpu as pltpu
from jax.sharding import PartitionSpec as P

NLON = 128
STEPS = 3
UNIT = STEPS * NLON
ROWS = 32
VMEM = 48 * 1024 * 1024


def stencil(c, east, west, north, south, coef):
    return coef[0] * c + coef[1] * east + coef[2] * west + coef[3] * north + coef[4] * south


def column_kernel(parts, sides, *refs):
    ins, tables, out = refs[: len(parts)], refs[len(parts)], refs[-1]
    for side, (names, first, count) in enumerate(sides):

        def source(line):
            part, at = divmod(line, STEPS)
            return ins[names[part]][at * NLON : (at + 1) * NLON, :]

        lines = count + 2 * STEPS
        got = {}
        for line in range(lines):
            got[0, line] = source(line)
            for step in range(1, STEPS + 1):
                mid = line - step
                if mid < step:
                    continue
                c = got[step - 1, mid]
                row = first + mid - 1
                value = stencil(
                    c,
                    pltpu.roll(c, NLON - 1, 0),
                    pltpu.roll(c, 1, 0),
                    got[step - 1, mid + 1],
                    got[step - 1, mid - 1],
                    [tables[k, row] for k in range(5)],
                )
                got.pop((step - 1, mid - 1))
                if step < STEPS:
                    got[step, mid] = value
                else:
                    at = sum(s[2] for s in sides[:side]) + mid - STEPS
                    out[at * NLON : (at + 1) * NLON, :] = value


def column_sweep(arrays, sides, width, coefs):
    total = sum(count for _, _, count in sides) * NLON
    in_specs = [
        pl.BlockSpec((UNIT, NLON), functools.partial(lambda i, r, c: (r, i + c), r=r, c=c)) for _, r, c in arrays
    ]
    in_specs.append(pl.BlockSpec(coefs.shape, lambda i: (0, 0, 0, 0)))
    work = total * width
    return pl.pallas_call(
        functools.partial(column_kernel, arrays, sides),
        grid=(width // NLON,),
        in_specs=in_specs,
        out_specs=pl.BlockSpec((total, NLON), lambda i: (0, i)),
        out_shape=jax.ShapeDtypeStruct((total, width), jnp.float32),
        compiler_params=pltpu.CompilerParams(vmem_limit_bytes=VMEM),
        cost_estimate=pl.CostEstimate(flops=work * 40, bytes_accessed=work * 12, transcendentals=0),
    )(*[a for a, _, _ in arrays], coefs)


def row_kernel(count, first, *refs):
    ins, coefs, out = refs[: count + 2], refs[count + 2], refs[-1]
    lines = (count + 2) * STEPS

    def group(g, carry):
        rows = pl.ds(pl.multiple_of(g * ROWS, ROWS), ROWS)
        got = {}
        for line in range(lines):
            part, at = divmod(line, STEPS)
            got[0, line] = ins[part][rows, at * NLON : (at + 1) * NLON]
            for step in range(1, STEPS + 1):
                mid = line - step
                if mid < step:
                    continue
                c = got[step - 1, mid]
                at = first + mid - 1
                value = stencil(
                    c.reshape(ROWS // 8, 8, NLON),
                    pltpu.roll(c, NLON - 1, 1).reshape(ROWS // 8, 8, NLON),
                    pltpu.roll(c, 1, 1).reshape(ROWS // 8, 8, NLON),
                    got[step - 1, mid + 1].reshape(ROWS // 8, 8, NLON),
                    got[step - 1, mid - 1].reshape(ROWS // 8, 8, NLON),
                    [coefs[k, at][None] for k in range(5)],
                ).reshape(ROWS, NLON)
                got.pop((step - 1, mid - 1))
                if step < STEPS:
                    got[step, mid] = value
                else:
                    to = mid - STEPS
                    out[rows, to * NLON : (to + 1) * NLON] = value
        return carry

    lax.fori_loop(0, out.shape[0] // ROWS, group, 0)


def row_sweep(arrays, first, coefs, out_rows, row_block, out_cols, col_block, buffer):
    block = NLON
    count = len(arrays) - 2
    rows = arrays[0][0].shape[0]
    in_specs = [pl.BlockSpec((block, UNIT), functools.partial(lambda i, c: (i, c), c=c)) for _, c in arrays]
    in_specs.append(pl.BlockSpec(coefs.shape, lambda i: (0, 0, 0, 0)))
    operands = [a for a, _ in arrays] + [coefs]
    aliases = {}
    if buffer is not None:
        in_specs.append(pl.BlockSpec(memory_space=pl.ANY))
        operands.append(buffer)
        aliases = {len(operands) - 1: 0}
    work = rows * count * UNIT
    return pl.pallas_call(
        functools.partial(row_kernel, count, first),
        grid=(rows // block,),
        in_specs=in_specs,
        out_specs=pl.BlockSpec((block, count * UNIT), lambda i: (row_block(i), col_block)),
        out_shape=jax.ShapeDtypeStruct((out_rows, out_cols), jnp.float32),
        input_output_aliases=aliases,
        compiler_params=pltpu.CompilerParams(vmem_limit_bytes=VMEM),
        cost_estimate=pl.CostEstimate(flops=work * 40, bytes_accessed=work * 12, transcendentals=0),
    )(*operands)


def exchange(first, last, axis):
    devices = lax.axis_size(axis)
    up = [(i, i + 1) for i in range(devices - 1)]
    down = [(j, i) for i, j in up]
    return lax.ppermute(last, axis, up), lax.ppermute(first, axis, down)


def coefficients(tables, offset, lines):
    east_wind, north_wind, diffuse_lon, diffuse_lat = tables
    made = jnp.stack(
        [
            1.0 - 2.0 * diffuse_lon - 2.0 * diffuse_lat,
            diffuse_lon - 0.5 * east_wind,
            diffuse_lon + 0.5 * east_wind,
            diffuse_lat - 0.5 * north_wind,
            diffuse_lat + 0.5 * north_wind,
        ]
    )
    edge = STEPS - 1
    made = jnp.pad(made, ((0, 0), (edge, edge), (0, 0)))
    return lax.dynamic_slice_in_dim(made, offset, lines + 2 * edge, 1)


def body(covariance, east_wind, north_wind, diffuse_lon, diffuse_lat):
    tables = (east_wind, north_wind, diffuse_lon, diffuse_lat)
    rows, cols = covariance.shape
    row_lines, col_lines = rows // NLON, cols // NLON
    row_units, col_units = rows // UNIT, cols // UNIT
    tiles = UNIT // NLON
    row_coefs = coefficients(tables, lax.axis_index("row") * row_lines, row_lines)
    row_coefs = jnp.broadcast_to(row_coefs[:, :, :, None], row_coefs.shape + (NLON,))
    col_coefs = coefficients(tables, lax.axis_index("col") * col_lines, col_lines)
    col_coefs = jnp.broadcast_to(col_coefs[:, :, None, :], col_coefs.shape[:2] + (8, NLON))

    if col_units == 1:
        pieces = [[0]]
    else:
        pieces = [[0, col_units - 1]]
        half = col_units // 2
        if col_units % 2 == 0 and col_units >= 6:
            pieces += [list(range(1, half + 1)), list(range(half + 1, col_units - 1))]
        elif col_units > 2:
            pieces += [list(range(1, col_units - 1))]

    def columns(units, low, high):
        parts = []
        for u in units:
            if parts and parts[-1][1] == u:
                parts[-1][1] = u + 1
            else:
                parts.append([u, u + 1])
        return jnp.concatenate([covariance[low:high, a * UNIT : b * UNIT] for a, b in parts], axis=1)

    halos = [exchange(columns(p, 0, UNIT), columns(p, rows - UNIT, rows), "row") for p in pieces]

    inner = None
    if row_units > 2:
        inner = column_sweep(
            [(covariance, r, 0) for r in range(row_units)],
            [(list(range(row_units)), STEPS, row_lines - 2 * STEPS)],
            cols,
            row_coefs,
        )

    outer = []
    where = {}
    for k, (units, (before, after)) in enumerate(zip(pieces, halos)):
        width = len(units) * UNIT
        if k == 0 and col_units > 1:
            own = columns(units, 0, rows)
            blocks = [(own, r, 0) for r in range(row_units)]
        else:
            blocks = [(covariance, r, units[0] * tiles) for r in range(row_units)]
        if row_units == 1:
            arrays = [(before, 0, 0), blocks[0], (after, 0, 0)]
            sides = [([0, 1, 2], 0, STEPS)]
        else:
            arrays = [(before, 0, 0), blocks[0], blocks[1], blocks[-2], blocks[-1], (after, 0, 0)]
            sides = [([0, 1, 2], 0, STEPS), ([3, 4, 5], row_lines - STEPS, STEPS)]
        outer.append(column_sweep(arrays, sides, width, row_coefs))
        for at, u in enumerate(units):
            where[u] = (k, at)

    out_blocks = rows // NLON
    halves = [list(range(col_units))]
    if len(pieces) == 3:
        halves = [list(range(half)), list(range(half, col_units))]

    edges = outer[0]
    outer_halo = exchange(edges[:, :UNIT], edges[:, -UNIT:], "col")
    out = None
    if inner is not None:
        inner_halo = exchange(inner[:, :UNIT], inner[:, cols - UNIT :], "col")
        arrays = [(inner_halo[0], 0)] + [(inner, u) for u in range(col_units)] + [(inner_halo[1], 0)]
        out = row_sweep(arrays, 0, col_coefs, rows, lambda i: i + tiles, cols, 0, out)

    def outer_row(i):
        return jnp.where(i < tiles, i, i + out_blocks - 2 * tiles) if row_units > 1 else i

    for h, units in enumerate(halves):
        arrays = []
        for u in [units[0] - 1] + units + [units[-1] + 1]:
            if u < 0:
                arrays.append((outer_halo[0], 0))
            elif u == col_units:
                arrays.append((outer_halo[1], 0))
            else:
                arrays.append((outer[where[u][0]], where[u][1]))
        out = row_sweep(arrays, units[0] * STEPS, col_coefs, rows, outer_row, cols, h, out)
    return out


def solution(mesh):
    return jax.shard_map(
        body,
        mesh=mesh,
        in_specs=(P("row", "col"), P(), P(), P(), P()),
        out_specs=P("row", "col"),
        check_vma=False,
    )
```

```python
import functools

import jax
import jax.numpy as jnp
from jax import lax
from jax.experimental import pallas as pl
from jax.experimental.pallas import tpu as pltpu
from jax.sharding import PartitionSpec as P

NLON = 128
STEPS = 3
UNIT = STEPS * NLON
WIDE = 256
BLOCK = 192
VMEM = 52 * 1024 * 1024


OFFSETS = [(y, x) for y in range(-STEPS, STEPS + 1) for x in range(-STEPS + abs(y), STEPS + 1 - abs(y))]


def power_kernel(east_wind, north_wind, diffuse_lon, diffuse_lat, plain, rolled):
    lon, lat = diffuse_lon[...], diffuse_lat[...]
    half_east, half_north = 0.5 * east_wind[...], 0.5 * north_wind[...]
    one = {
        (0, 0): 1.0 - 2.0 * lon - 2.0 * lat,
        (0, 1): lon - half_east,
        (0, -1): lon + half_east,
        (1, 0): lat - half_north,
        (-1, 0): lat + half_north,
    }
    lines = lon.shape[0]
    line = lax.broadcasted_iota(jnp.int32, lon.shape, 0)

    def seen(field, y, x):
        if x:
            return pltpu.roll(field, -x % NLON, 1)
        if y:
            edge = lines - 1 if y > 0 else 0
            return jnp.where(line == edge, 0.0, pltpu.roll(field, -y % lines, 0))
        return field

    power = dict(one)
    for _ in range(STEPS - 1):
        made = {}
        for (y, x), field in power.items():
            for (sy, sx), scale in one.items():
                term = scale * seen(field, sy, sx)
                at = (y + sy, x + sx)
                made[at] = made[at] + term if at in made else term
        power = made
    for k, (y, x) in enumerate(OFFSETS):
        plain[k] = power[y, x]
        rolled[k] = pltpu.roll(power[y, x], x % NLON, 1)


def powers(tables):
    shape = jax.ShapeDtypeStruct((len(OFFSETS),) + tables[0].shape, jnp.float32)
    return pl.pallas_call(
        power_kernel,
        out_shape=(shape, shape),
        compiler_params=pltpu.CompilerParams(vmem_limit_bytes=VMEM),
        cost_estimate=pl.CostEstimate(flops=10**7, bytes_accessed=10**7, transcendentals=0),
    )(*tables)


def split(value):
    high = value.astype(jnp.bfloat16)
    return high, (value - high.astype(jnp.float32)).astype(jnp.bfloat16)


def block_kernel(made, transposed, offset, table, out):
    base = offset[0] + pl.program_id(0) * made
    sub = lax.broadcasted_iota(jnp.int32, (NLON, NLON), 0)
    lane = lax.broadcasted_iota(jnp.int32, (NLON, NLON), 1)
    away = (sub - lane if transposed else lane - sub) & (NLON - 1)
    read = made + 2 * STEPS
    for a in range(made):
        for b in range(read):
            y = b - a - STEPS
            value = jnp.zeros((NLON, NLON), jnp.float32)
            for k, (oy, x) in enumerate(OFFSETS):
                if oy == y:
                    line = table[k, pl.ds(base + a, 1), :]
                    value = jnp.where(away == x % NLON, jnp.broadcast_to(line, (NLON, NLON)), value)
            high, low = split(value)
            mine, theirs = slice(a * NLON, (a + 1) * NLON), slice(b * NLON, (b + 1) * NLON)
            if transposed:
                out[0, theirs, mine] = high
                out[0, slice((read + b) * NLON, (read + b + 1) * NLON), mine] = low
            else:
                out[0, mine, theirs] = high
                out[0, slice((made + a) * NLON, (made + a + 1) * NLON), theirs] = low


def blocks_of(table, offset, groups, made, transposed):
    read = made + 2 * STEPS
    shape = (2 * read * NLON, made * NLON) if transposed else (2 * made * NLON, read * NLON)
    return pl.pallas_call(
        functools.partial(block_kernel, made, transposed),
        grid=(groups,),
        in_specs=[
            pl.BlockSpec(memory_space=pltpu.SMEM),
            pl.BlockSpec(table.shape, lambda i: (0, 0, 0)),
        ],
        out_specs=pl.BlockSpec((1,) + shape, lambda i: (i, 0, 0)),
        out_shape=jax.ShapeDtypeStruct((groups,) + shape, jnp.bfloat16),
        compiler_params=pltpu.CompilerParams(vmem_limit_bytes=VMEM),
        cost_estimate=pl.CostEstimate(flops=10**7, bytes_accessed=2 * 10**7, transcendentals=0),
    )(offset.reshape(1).astype(jnp.int32), table)


def dot(a, b):
    return jnp.dot(a, b, preferred_element_type=jnp.float32)


def column_kernel(sides, *refs):
    ins, tables, out, high, low = refs[:-4], refs[-4], refs[-3], refs[-2], refs[-1]
    for n, ref in enumerate(ins):
        rows = slice(n * UNIT, (n + 1) * UNIT)
        high[rows, :], low[rows, :] = split(ref[...])
    for at, (start, group) in enumerate(sides):
        rows = slice(start * UNIT, (start + 3) * UNIT)
        both = dot(tables[group], high[rows, :])
        other = dot(tables[group, :UNIT, :], low[rows, :])
        out[at * UNIT : (at + 1) * UNIT, :] = both[:UNIT] + (both[UNIT:] + other)


def column_sweep(arrays, sides, width, tables):
    total = len(sides) * UNIT
    tile = WIDE if all(n % WIDE == 0 for n in [width] + [c for _, _, c in arrays]) else UNIT
    in_specs = [
        pl.BlockSpec((UNIT, tile), functools.partial(lambda i, r, c: (r, i + c), r=r, c=c // tile))
        for _, r, c in arrays
    ]
    in_specs.append(pl.BlockSpec(tables.shape, lambda i: (0, 0, 0), pipeline_mode=pl.Buffered(1)))
    scratch = pltpu.VMEM((len(arrays) * UNIT, tile), jnp.bfloat16)
    work = total * width
    return pl.pallas_call(
        functools.partial(column_kernel, sides),
        grid=(width // tile,),
        in_specs=in_specs,
        out_specs=pl.BlockSpec((total, tile), lambda i: (0, i)),
        out_shape=jax.ShapeDtypeStruct((total, width), jnp.float32),
        scratch_shapes=[scratch, scratch],
        compiler_params=pltpu.CompilerParams(vmem_limit_bytes=VMEM),
        cost_estimate=pl.CostEstimate(flops=work * 2 * 1152 * 3, bytes_accessed=work * 12, transcendentals=0),
    )(*[a for a, _, _ in arrays], tables)


def row_kernel(count, *refs):
    ins, tables, out, both = refs[: count + 2], refs[count + 2], refs[-2], refs[-1]
    rows = out.shape[0]
    read = (2 + 2 * STEPS) * NLON
    for n, ref in enumerate(ins):
        cols = slice(n * UNIT, (n + 1) * UNIT)
        both[:rows, cols], both[rows:, cols] = split(ref[...])
    for pair in range(count * STEPS // 2):
        cols = slice(pair * 2 * NLON, pair * 2 * NLON + read)
        first = dot(both[:, cols], tables[pair, :read, :])
        other = dot(both[:rows, cols], tables[pair, read:, :])
        out[:, pair * 2 * NLON : (pair + 1) * 2 * NLON] = first[:rows] + (first[rows:] + other)


def row_sweep(arrays, part, tables, out_rows, row_block, out_cols, col_block, buffer):
    count = len(arrays) - 2
    rows = arrays[0][0].shape[0]
    pairs = count * STEPS // 2
    in_specs = [pl.BlockSpec((BLOCK, UNIT), functools.partial(lambda i, c: (i, c), c=c)) for _, c in arrays]
    in_specs.append(
        pl.BlockSpec((pairs,) + tables.shape[1:], lambda i: (part, 0, 0), pipeline_mode=pl.Buffered(1))
    )
    operands = [a for a, _ in arrays] + [tables]
    aliases = {}
    if buffer is not None:
        in_specs.append(pl.BlockSpec(memory_space=pl.ANY))
        operands.append(buffer)
        aliases = {len(operands) - 1: 0}
    work = rows * count * UNIT
    return pl.pallas_call(
        functools.partial(row_kernel, count),
        grid=(rows // BLOCK,),
        in_specs=in_specs,
        out_specs=pl.BlockSpec((BLOCK, count * UNIT), lambda i: (row_block(i), col_block)),
        out_shape=jax.ShapeDtypeStruct((out_rows, out_cols), jnp.float32),
        input_output_aliases=aliases,
        scratch_shapes=[pltpu.VMEM((2 * BLOCK, len(arrays) * UNIT), jnp.bfloat16)],
        compiler_params=pltpu.CompilerParams(vmem_limit_bytes=VMEM),
        cost_estimate=pl.CostEstimate(flops=work * 2 * 1024 * 3, bytes_accessed=work * 12, transcendentals=0),
    )(*operands)


def exchange(first, last, axis):
    devices = lax.axis_size(axis)
    up = [(i, i + 1) for i in range(devices - 1)]
    down = [(j, i) for i, j in up]
    return lax.ppermute(last, axis, up), lax.ppermute(first, axis, down)


def body(covariance, east_wind, north_wind, diffuse_lon, diffuse_lat):
    tables = (east_wind, north_wind, diffuse_lon, diffuse_lat)
    rows, cols = covariance.shape
    row_lines, col_lines = rows // NLON, cols // NLON
    row_units, col_units = rows // UNIT, cols // UNIT
    plain, rolled = powers(tables)
    row_tables = blocks_of(rolled, lax.axis_index("row") * row_lines, row_units, STEPS, False)
    col_tables = blocks_of(plain, lax.axis_index("col") * col_lines, col_lines // 2, 2, True)

    if col_units == 1:
        pieces = [[0]]
    else:
        pieces = [[0, col_units - 1]]
        half = col_units // 2
        if col_units % 2 == 0 and col_units >= 6:
            pieces += [list(range(1, half + 1)), list(range(half + 1, col_units - 1))]
        elif col_units > 2:
            pieces += [list(range(1, col_units - 1))]

    def columns(units, low, high):
        parts = []
        for u in units:
            if parts and parts[-1][1] == u:
                parts[-1][1] = u + 1
            else:
                parts.append([u, u + 1])
        return jnp.concatenate([covariance[low:high, a * UNIT : b * UNIT] for a, b in parts], axis=1)

    halos = [exchange(columns(p, 0, UNIT), columns(p, rows - UNIT, rows), "row") for p in pieces]

    inner = None
    if row_units > 2:
        inner = column_sweep(
            [(covariance, r, 0) for r in range(row_units)],
            [(u, u + 1) for u in range(row_units - 2)],
            cols,
            row_tables,
        )

    outer = []
    where = {}
    for k, (units, (before, after)) in enumerate(zip(pieces, halos)):
        width = len(units) * UNIT
        if k == 0 and col_units > 1:
            own = columns(units, 0, rows)
            blocks = [(own, r, 0) for r in range(row_units)]
        else:
            blocks = [(covariance, r, units[0] * UNIT) for r in range(row_units)]
        if row_units == 1:
            arrays = [(before, 0, 0), blocks[0], (after, 0, 0)]
            sides = [(0, 0)]
        else:
            arrays = [(before, 0, 0), blocks[0], blocks[1], blocks[-2], blocks[-1], (after, 0, 0)]
            sides = [(0, 0), (3, row_units - 1)]
        outer.append(column_sweep(arrays, sides, width, row_tables))
        for at, u in enumerate(units):
            where[u] = (k, at)

    out_blocks, tiles = rows // BLOCK, UNIT // BLOCK
    halves = [list(range(col_units))]
    if len(pieces) == 3:
        halves = [list(range(half)), list(range(half, col_units))]

    edges = outer[0]
    outer_halo = exchange(edges[:, :UNIT], edges[:, -UNIT:], "col")
    out = None
    if inner is not None:
        inner_halo = exchange(inner[:, :UNIT], inner[:, cols - UNIT :], "col")
        arrays = [(inner_halo[0], 0)] + [(inner, u) for u in range(col_units)] + [(inner_halo[1], 0)]
        out = row_sweep(arrays, 0, col_tables, rows, lambda i: i + tiles, cols, 0, out)

    def outer_row(i):
        return jnp.where(i < tiles, i, i + out_blocks - 2 * tiles) if row_units > 1 else i

    for h, units in enumerate(halves):
        arrays = []
        for u in [units[0] - 1] + units + [units[-1] + 1]:
            if u < 0:
                arrays.append((outer_halo[0], 0))
            elif u == col_units:
                arrays.append((outer_halo[1], 0))
            else:
                arrays.append((outer[where[u][0]], where[u][1]))
        out = row_sweep(arrays, h, col_tables, rows, outer_row, cols, h, out)
    return out


def solution(mesh):
    return jax.shard_map(
        body,
        mesh=mesh,
        in_specs=(P("row", "col"), P(), P(), P(), P()),
        out_specs=P("row", "col"),
        check_vma=False,
    )
```

```python
import functools

import jax
import jax.numpy as jnp
from jax import lax
from jax.experimental import pallas as pl
from jax.experimental.pallas import tpu as pltpu
from jax.sharding import PartitionSpec as P

NLON = 128
STEPS = 3
UNIT = STEPS * NLON
WIDE = 256
BLOCK = 192
VMEM = 52 * 1024 * 1024


OFFSETS = [(y, x) for y in range(-STEPS, STEPS + 1) for x in range(-STEPS + abs(y), STEPS + 1 - abs(y))]


def power_kernel(east_wind, north_wind, diffuse_lon, diffuse_lat, plain, rolled):
    lon, lat = diffuse_lon[...], diffuse_lat[...]
    half_east, half_north = 0.5 * east_wind[...], 0.5 * north_wind[...]
    one = {
        (0, 0): 1.0 - 2.0 * lon - 2.0 * lat,
        (0, 1): lon - half_east,
        (0, -1): lon + half_east,
        (1, 0): lat - half_north,
        (-1, 0): lat + half_north,
    }
    lines = lon.shape[0]
    line = lax.broadcasted_iota(jnp.int32, lon.shape, 0)

    def seen(field, y, x):
        if x:
            return pltpu.roll(field, -x % NLON, 1)
        if y:
            edge = lines - 1 if y > 0 else 0
            return jnp.where(line == edge, 0.0, pltpu.roll(field, -y % lines, 0))
        return field

    power = dict(one)
    for _ in range(STEPS - 1):
        made = {}
        for (y, x), field in power.items():
            for (sy, sx), scale in one.items():
                term = scale * seen(field, sy, sx)
                at = (y + sy, x + sx)
                made[at] = made[at] + term if at in made else term
        power = made
    for k, (y, x) in enumerate(OFFSETS):
        plain[k] = power[y, x]
        rolled[k] = pltpu.roll(power[y, x], x % NLON, 1)


def powers(tables):
    shape = jax.ShapeDtypeStruct((len(OFFSETS),) + tables[0].shape, jnp.float32)
    return pl.pallas_call(
        power_kernel,
        out_shape=(shape, shape),
        compiler_params=pltpu.CompilerParams(vmem_limit_bytes=VMEM),
        cost_estimate=pl.CostEstimate(flops=10**7, bytes_accessed=10**7, transcendentals=0),
    )(*tables)


def split(value):
    high = value.astype(jnp.bfloat16)
    return high, (value - high.astype(jnp.float32)).astype(jnp.bfloat16)


def block_kernel(made, transposed, offset, table, out):
    base = offset[0] + pl.program_id(0) * made
    sub = lax.broadcasted_iota(jnp.int32, (NLON, NLON), 0)
    lane = lax.broadcasted_iota(jnp.int32, (NLON, NLON), 1)
    away = (sub - lane if transposed else lane - sub) & (NLON - 1)
    read = made + 2 * STEPS
    for a in range(made):
        for b in range(read):
            y = b - a - STEPS
            value = jnp.zeros((NLON, NLON), jnp.float32)
            for k, (oy, x) in enumerate(OFFSETS):
                if oy == y:
                    line = table[k, pl.ds(base + a, 1), :]
                    value = jnp.where(away == x % NLON, jnp.broadcast_to(line, (NLON, NLON)), value)
            high, low = split(value)
            mine, theirs = slice(a * NLON, (a + 1) * NLON), slice(b * NLON, (b + 1) * NLON)
            if transposed:
                out[0, theirs, mine] = high
                out[0, slice((read + b) * NLON, (read + b + 1) * NLON), mine] = low
            else:
                out[0, mine, theirs] = high
                out[0, slice((made + a) * NLON, (made + a + 1) * NLON), theirs] = low


def blocks_of(table, offset, groups, made, transposed):
    read = made + 2 * STEPS
    shape = (2 * read * NLON, made * NLON) if transposed else (2 * made * NLON, read * NLON)
    return pl.pallas_call(
        functools.partial(block_kernel, made, transposed),
        grid=(groups,),
        in_specs=[
            pl.BlockSpec(memory_space=pltpu.SMEM),
            pl.BlockSpec(table.shape, lambda i: (0, 0, 0)),
        ],
        out_specs=pl.BlockSpec((1,) + shape, lambda i: (i, 0, 0)),
        out_shape=jax.ShapeDtypeStruct((groups,) + shape, jnp.bfloat16),
        compiler_params=pltpu.CompilerParams(vmem_limit_bytes=VMEM),
        cost_estimate=pl.CostEstimate(flops=10**7, bytes_accessed=2 * 10**7, transcendentals=0),
    )(offset.reshape(1).astype(jnp.int32), table)


def dot(a, b):
    return jnp.dot(a, b, preferred_element_type=jnp.float32)


def stencil(c, east, west, north, south, coef):
    return coef[0] * c + coef[1] * east + coef[2] * west + coef[3] * north + coef[4] * south


def column_kernel(parts, sides, *refs):
    ins, tables, out = refs[: len(parts)], refs[len(parts)], refs[-1]
    for side, (names, first, count) in enumerate(sides):

        def source(line):
            part, at = divmod(line, STEPS)
            return ins[names[part]][at * NLON : (at + 1) * NLON, :]

        lines = count + 2 * STEPS
        got = {}
        for line in range(lines):
            got[0, line] = source(line)
            for step in range(1, STEPS + 1):
                mid = line - step
                if mid < step:
                    continue
                c = got[step - 1, mid]
                row = first + mid - 1
                value = stencil(
                    c,
                    pltpu.roll(c, NLON - 1, 0),
                    pltpu.roll(c, 1, 0),
                    got[step - 1, mid + 1],
                    got[step - 1, mid - 1],
                    [tables[k, row] for k in range(5)],
                )
                got.pop((step - 1, mid - 1))
                if step < STEPS:
                    got[step, mid] = value
                else:
                    at = sum(s[2] for s in sides[:side]) + mid - STEPS
                    out[at * NLON : (at + 1) * NLON, :] = value


def column_sweep(arrays, sides, width, coefs):
    total = sum(count for _, _, count in sides) * NLON
    in_specs = [
        pl.BlockSpec((UNIT, NLON), functools.partial(lambda i, r, c, skip: (r, jnp.where(i < UNIT // NLON, i + c, i + c + skip)), r=r, c=c, skip=skip)) for _, r, c, skip in arrays
    ]
    in_specs.append(pl.BlockSpec(coefs.shape, lambda i: (0, 0, 0, 0)))
    work = total * width
    return pl.pallas_call(
        functools.partial(column_kernel, arrays, sides),
        grid=(width // NLON,),
        in_specs=in_specs,
        out_specs=pl.BlockSpec((total, NLON), lambda i: (0, i)),
        out_shape=jax.ShapeDtypeStruct((total, width), jnp.float32),
        compiler_params=pltpu.CompilerParams(vmem_limit_bytes=VMEM),
        cost_estimate=pl.CostEstimate(flops=work * 40, bytes_accessed=work * 12, transcendentals=0),
    )(*[a[0] for a in arrays], coefs)


def row_kernel(count, *refs):
    ins, tables, out, both = refs[: count + 2], refs[count + 2], refs[-2], refs[-1]
    rows = out.shape[0]
    read = (2 + 2 * STEPS) * NLON
    for n, ref in enumerate(ins):
        cols = slice(n * UNIT, (n + 1) * UNIT)
        both[:rows, cols], both[rows:, cols] = split(ref[...])
    for pair in range(count * STEPS // 2):
        cols = slice(pair * 2 * NLON, pair * 2 * NLON + read)
        first = dot(both[:, cols], tables[pair, :read, :])
        other = dot(both[:rows, cols], tables[pair, read:, :])
        out[:, pair * 2 * NLON : (pair + 1) * 2 * NLON] = first[:rows] + (first[rows:] + other)


def row_sweep(arrays, part, tables, out_rows, row_block, out_cols, col_block, buffer):
    count = len(arrays) - 2
    rows = arrays[0][0].shape[0]
    pairs = count * STEPS // 2
    in_specs = [pl.BlockSpec((BLOCK, UNIT), functools.partial(lambda i, c: (i, c), c=c)) for _, c in arrays]
    in_specs.append(
        pl.BlockSpec((pairs,) + tables.shape[1:], lambda i: (part, 0, 0), pipeline_mode=pl.Buffered(1))
    )
    operands = [a for a, _ in arrays] + [tables]
    aliases = {}
    if buffer is not None:
        in_specs.append(pl.BlockSpec(memory_space=pl.ANY))
        operands.append(buffer)
        aliases = {len(operands) - 1: 0}
    work = rows * count * UNIT
    return pl.pallas_call(
        functools.partial(row_kernel, count),
        grid=(rows // BLOCK,),
        in_specs=in_specs,
        out_specs=pl.BlockSpec((BLOCK, count * UNIT), lambda i: (row_block(i), col_block)),
        out_shape=jax.ShapeDtypeStruct((out_rows, out_cols), jnp.float32),
        input_output_aliases=aliases,
        scratch_shapes=[pltpu.VMEM((2 * BLOCK, len(arrays) * UNIT), jnp.bfloat16)],
        compiler_params=pltpu.CompilerParams(vmem_limit_bytes=VMEM),
        cost_estimate=pl.CostEstimate(flops=work * 40, bytes_accessed=work * 12, transcendentals=0),
    )(*operands)


def exchange(first, last, axis):
    devices = lax.axis_size(axis)
    up = [(i, i + 1) for i in range(devices - 1)]
    down = [(j, i) for i, j in up]
    return lax.ppermute(last, axis, up), lax.ppermute(first, axis, down)


def coefficients(tables, offset, lines):
    east_wind, north_wind, diffuse_lon, diffuse_lat = tables
    made = jnp.stack(
        [
            1.0 - 2.0 * diffuse_lon - 2.0 * diffuse_lat,
            diffuse_lon - 0.5 * east_wind,
            diffuse_lon + 0.5 * east_wind,
            diffuse_lat - 0.5 * north_wind,
            diffuse_lat + 0.5 * north_wind,
        ]
    )
    edge = STEPS - 1
    made = jnp.pad(made, ((0, 0), (edge, edge), (0, 0)))
    return lax.dynamic_slice_in_dim(made, offset, lines + 2 * edge, 1)


def body(covariance, east_wind, north_wind, diffuse_lon, diffuse_lat):
    tables = (east_wind, north_wind, diffuse_lon, diffuse_lat)
    rows, cols = covariance.shape
    row_lines, col_lines = rows // NLON, cols // NLON
    row_units, col_units = rows // UNIT, cols // UNIT
    row_coefs = coefficients(tables, lax.axis_index("row") * row_lines, row_lines)
    row_coefs = jnp.broadcast_to(row_coefs[:, :, :, None], row_coefs.shape + (NLON,))
    plain, _ = powers(tables)
    col_tables = blocks_of(plain, lax.axis_index("col") * col_lines, col_lines // 2, 2, True)

    if col_units == 1:
        pieces = [[0]]
    else:
        pieces = [[0, col_units - 1]]
        half = col_units // 2
        if col_units % 2 == 0 and col_units >= 6:
            pieces += [list(range(1, half + 1)), list(range(half + 1, col_units - 1))]
        elif col_units > 2:
            pieces += [list(range(1, col_units - 1))]

    def columns(units, low, high):
        parts = []
        for u in units:
            if parts and parts[-1][1] == u:
                parts[-1][1] = u + 1
            else:
                parts.append([u, u + 1])
        return jnp.concatenate([covariance[low:high, a * UNIT : b * UNIT] for a, b in parts], axis=1)

    halos = [exchange(columns(p, 0, UNIT), columns(p, rows - UNIT, rows), "row") for p in pieces]

    inner = None
    if row_units > 2:
        inner = column_sweep(
            [(covariance, r, 0, 0) for r in range(row_units)],
            [(list(range(row_units)), STEPS, row_lines - 2 * STEPS)],
            cols,
            row_coefs,
        )

    outer = []
    where = {}
    for k, (units, (before, after)) in enumerate(zip(pieces, halos)):
        width = len(units) * UNIT
        skip = (cols - 2 * UNIT) // NLON if k == 0 and col_units > 1 else 0
        blocks = [(covariance, r, units[0] * (UNIT // NLON), skip) for r in range(row_units)]
        if row_units == 1:
            arrays = [(before, 0, 0, 0), blocks[0], (after, 0, 0, 0)]
            sides = [([0, 1, 2], 0, STEPS)]
        else:
            arrays = [(before, 0, 0, 0), blocks[0], blocks[1], blocks[-2], blocks[-1], (after, 0, 0, 0)]
            sides = [([0, 1, 2], 0, STEPS), ([3, 4, 5], row_lines - STEPS, STEPS)]
        outer.append(column_sweep(arrays, sides, width, row_coefs))
        for at, u in enumerate(units):
            where[u] = (k, at)

    out_blocks, tiles = rows // BLOCK, UNIT // BLOCK
    halves = [list(range(col_units))]
    if len(pieces) == 3:
        halves = [list(range(half)), list(range(half, col_units))]

    edges = outer[0]
    outer_halo = exchange(edges[:, :UNIT], edges[:, -UNIT:], "col")
    out = None
    if inner is not None:
        inner_halo = exchange(inner[:, :UNIT], inner[:, cols - UNIT :], "col")
        arrays = [(inner_halo[0], 0)] + [(inner, u) for u in range(col_units)] + [(inner_halo[1], 0)]
        out = row_sweep(arrays, 0, col_tables, rows, lambda i: i + tiles, cols, 0, out)

    def outer_row(i):
        return jnp.where(i < tiles, i, i + out_blocks - 2 * tiles) if row_units > 1 else i

    for h, units in enumerate(halves):
        arrays = []
        for u in [units[0] - 1] + units + [units[-1] + 1]:
            if u < 0:
                arrays.append((outer_halo[0], 0))
            elif u == col_units:
                arrays.append((outer_halo[1], 0))
            else:
                arrays.append((outer[where[u][0]], where[u][1]))
        out = row_sweep(arrays, h, col_tables, rows, outer_row, cols, h, out)
    return out


def solution(mesh):
    return jax.shard_map(
        body,
        mesh=mesh,
        in_specs=(P("row", "col"), P(), P(), P(), P()),
        out_specs=P("row", "col"),
        check_vma=False,
    )
```
